256 devices in a mesh: seg: 32 (over y, z), chan: 8 (over x, core).
Axes of the slice: x: 4, y: 4, z: 8, core: 2. Of those that a mesh axis runs over, the one named last changes fastest.
Arguments:
- ref_signals: bfloat16 [32, 524288], P('chan', 'seg'), may hold values from -6 to 6
- responses: bfloat16 [1024, 524288], P('chan', 'seg'), may hold values from -48 to 48
Outputs:
- transfer: float32 [512, 2, 32, 1024], P('seg', None, None, 'chan')
The draws below stay inside these ranges and needn't reach their ends.
All inputs are finite; a program needn't handle non-finite values.
Results may differ from the reference program's by a relative error of at most 0.006.
Values may be sent and summed in bfloat16 or wider, within the bound.
No kernel may reach another device: no remote copies, remote signals or barrier semaphores. Data moves between devices by JAX's collectives and lax.ppermute only.
A program may use at most 128 MiB of HBM per device.

```python
import jax
import jax.numpy as jnp
from jax import lax

L = 2048
FB = 512
R = 32
C = 1024
SEGS = 256
TIME = 524288


def shard_levels(rng, dims, cuts, least, largest):
    def one(position, blocks):
        draws = jax.random.uniform(jax.random.fold_in(jax.random.fold_in(rng, 6), position), (blocks,), jnp.float32, least / len(cuts), largest / len(cuts))
        return jnp.repeat(jnp.exp(draws), dims[position] // blocks).reshape((-1,) + (1,) * (len(dims) - position - 1))

    gain = one(*cuts[0])
    for cut in cuts[1:]:
        gain = gain * one(*cut)
    return gain


def centred(key, extent, scale, most, shards=(), held_as=jnp.bfloat16):
    gain = shard_levels(key, extent, shards, -0.22, 0.18) if shards else 1.0
    values = jax.random.normal(key, extent, jnp.float32) * scale * gain
    return jnp.minimum(jnp.maximum(values, -most), most).astype(held_as)


def setup_inputs(seed: int = 0) -> dict:
    seeds = jax.random.split(jax.random.key(seed), 3)
    return {
        "ref_signals": centred(seeds[0], (R, TIME), 1.0, 6.0, ((0, 8), (1, 32))),
        "responses": centred(seeds[1], (C, TIME), 8.0, 48.0, ((0, 8), (1, 32))),
    }


def dft_table(length, line_count):
    sample_idx = jnp.arange(length, dtype=jnp.int32)[:, None]
    line_idx = jnp.arange(line_count, dtype=jnp.int32)[None, :]
    phases = (sample_idx * line_idx % length).astype(jnp.float32) * (2.0 * jnp.pi / length)
    window = 0.5 - 0.5 * jnp.cos(jnp.arange(length, dtype=jnp.int32).astype(jnp.float32) * (2.0 * jnp.pi / length))
    cos_part = window[:, None] * jnp.cos(phases)
    sin_part = -window[:, None] * jnp.sin(phases)
    return jnp.stack([cos_part, sin_part], axis=2).reshape(length, 2 * line_count).astype(jnp.bfloat16)

def contract(left_op, right_op):
    return jnp.einsum('af,bf->fab', left_op.astype(jnp.float32), right_op.astype(jnp.float32), precision=lax.Precision.HIGHEST)

def reference(ref_signals, responses):
    kernel = dft_table(L, FB).astype(jnp.float32)

    def accumulate(totals, seg_index):
        auto_sums, cross_sums = totals
        ref_seg = lax.dynamic_slice_in_dim(ref_signals, (seg_index * L).astype(jnp.int32), L, 1)
        resp_seg = lax.dynamic_slice_in_dim(responses, (seg_index * L).astype(jnp.int32), L, 1)
        ref_lines = jnp.dot(ref_seg.astype(jnp.float32), kernel, precision=lax.Precision.HIGHEST).astype(jnp.bfloat16)
        resp_lines = jnp.dot(resp_seg.astype(jnp.float32), kernel, precision=lax.Precision.HIGHEST).astype(jnp.bfloat16)
        ref_split = ref_lines.reshape(R, FB, 2)
        resp_split = resp_lines.reshape(C, FB, 2)
        ref_real, ref_imag = (ref_split[:, :, 0], ref_split[:, :, 1])
        resp_real, resp_imag = (resp_split[:, :, 0], resp_split[:, :, 1])
        auto_term = jnp.stack([contract(ref_real, ref_real) + contract(ref_imag, ref_imag), contract(ref_real, ref_imag) - contract(ref_imag, ref_real)], 1)
        cross_term = jnp.stack([contract(ref_real, resp_real) + contract(ref_imag, resp_imag), contract(ref_real, resp_imag) - contract(ref_imag, resp_real)], 1)
        return ((auto_sums + auto_term, cross_sums + cross_term), None)
    start_totals = (jnp.zeros((FB, 2, R, R), jnp.float32), jnp.zeros((FB, 2, R, C), jnp.float32))
    (auto_sums, cross_sums), unused = lax.scan(accumulate, start_totals, jnp.arange(SEGS, dtype=jnp.int32))
    return solve_lines(auto_sums, cross_sums)

def solve_lines(auto_sums, cross_sums):
    real_part = auto_sums[:, 0]
    imag_part = auto_sums[:, 1]
    real_form = jnp.concatenate([jnp.concatenate([real_part, -imag_part], 2), jnp.concatenate([imag_part, real_part], 2)], 1)
    right_side = jnp.concatenate([cross_sums[:, 0], cross_sums[:, 1]], 1)
    factor = jnp.linalg.cholesky(real_form)
    solved = jax.scipy.linalg.cho_solve((factor, True), right_side)
    return solved.reshape(solved.shape[0], 2, solved.shape[1] // 2, solved.shape[2])
```

```python
import jax
import jax.numpy as jnp
import numpy as np
from jax import lax
from jax.experimental import pallas as pl
from jax.experimental.pallas import tpu as pltpu
from jax.sharding import PartitionSpec as P

L = 2048
FB = 512
NSEG = 32
NCHAN = 8
S = 8
LN = FB // NSEG
R = 32
RL = R // NCHAN
CL = 128
ROWS = 2 * S
DEPTH = NSEG * ROWS


def dft_table():
    n = np.arange(L, dtype=np.int64)[None, :]
    k = np.arange(FB, dtype=np.int64)[:, None]
    phase = (n * k % L) * (2.0 * np.pi / L)
    window = 0.5 - 0.5 * np.cos(n * (2.0 * np.pi / L))
    table = np.stack([window * np.cos(phase), -window * np.sin(phase)], axis=1)
    return jnp.asarray(table.reshape(2 * FB, L), dtype=jnp.bfloat16)


def transform_kernel(table_ref, resp_ref, ref_ref, out_ref, mixed):
    step = pl.program_id(0)
    block = resp_ref[...]
    pair = jnp.concatenate([block[:, :L], block[:, L:]], axis=0)
    for q in range(4):
        rows = slice(q * 256, (q + 1) * 256)
        lines = lax.dot_general(
            table_ref[rows, :], pair, (((1,), (1,)), ((), ())), preferred_element_type=jnp.float32
        )
        for i in range(2):
            mixed[pl.ds(q * 256 * S + 2 * step + i, 256, stride=S), :] = lines[:, i * CL : (i + 1) * CL]

    @pl.when(step == S // 2 - 1)
    def _():
        for d in range(NSEG):
            rows = LN * ROWS
            out_ref[d, 0:rows, :] = mixed[d * rows : (d + 1) * rows, :].astype(jnp.bfloat16)
        spec = lax.dot_general(
            ref_ref[...], table_ref[...], (((1,), (1,)), ((), ())), preferred_element_type=jnp.float32
        )
        for d in range(NSEG):
            parts = [spec[r * S : (r + 1) * S, d * 2 * LN : (d + 1) * 2 * LN] for r in range(RL)]
            tile = jnp.concatenate(parts, axis=1)
            out_ref[d, LN * ROWS :, :] = jnp.concatenate([tile, jnp.zeros_like(tile)], axis=0).astype(jnp.bfloat16)


def transform(table, responses, refs):
    return pl.pallas_call(
        transform_kernel,
        grid=(S // 2,),
        in_specs=[
            pl.BlockSpec((2 * FB, L), lambda i: (0, 0)),
            pl.BlockSpec((CL, 2 * L), lambda i: (0, i)),
            pl.BlockSpec((RL * S, L), lambda i: (0, 0)),
        ],
        out_specs=pl.BlockSpec((NSEG, (LN + 1) * ROWS, CL), lambda i: (0, 0, 0)),
        out_shape=jax.ShapeDtypeStruct((NSEG, (LN + 1) * ROWS, CL), jnp.bfloat16),
        scratch_shapes=[pltpu.VMEM((2 * FB * S, CL), jnp.float32)],
        compiler_params=pltpu.CompilerParams(vmem_limit_bytes=48 * 1024 * 1024),
    )(table, responses, refs)


def spots(shape, target):
    row = lax.broadcasted_iota(jnp.int32, shape, 0)
    column = lax.broadcasted_iota(jnp.int32, shape, 1)
    return jnp.where(column == target(row), 1.0, 0.0).astype(jnp.bfloat16)


def exact(left, right, dims):
    return lax.dot_general(left, right, (dims, ((), ())), preferred_element_type=jnp.float32).astype(jnp.bfloat16)


def solve_kernel(resp_ref, ref_ref, out_ref, auto, cross):
    wide = jnp.concatenate([ref_ref[c] for c in range(NCHAN)], axis=1)
    halves = []
    for part in range(2):
        pick = spots(
            (LN * R, NCHAN * 128),
            lambda i: (i // RL) % NCHAN * 128 + i % RL * (2 * LN) + i // R * 2 + part,
        )
        halves.append(exact(pick, wide, ((1,), (1,))))
    real, imag = halves
    put = [spots((NSEG * S, DEPTH), lambda i: i // S * ROWS + part * S + i % S) for part in range(2)]
    inner = ((1,), (0,))
    upper = exact(real, put[0], inner) + exact(imag, put[1], inner)
    lower = exact(real, put[1], inner) - exact(imag, put[0], inner)
    for k in range(LN):
        rows = slice(k * R, (k + 1) * R)
        both = jnp.concatenate([upper[rows], lower[rows]], axis=0)
        lines = resp_ref[:, k * ROWS : (k + 1) * ROWS, :].reshape(DEPTH, CL)
        cross[k] = jnp.dot(both, lines, preferred_element_type=jnp.float32)
        own = lax.dot_general(both, upper[rows], (((1,), (1,)), ((), ())), preferred_element_type=jnp.float32)
        auto[k] = jnp.concatenate([own[:R], own[R:]], axis=1)
    row = lax.broadcasted_iota(jnp.int32, (1, R, 1), 1)
    for k in range(R):
        a = auto[...]
        pivot = auto[:, k : k + 1, :]
        inverse = 1.0 / pivot[:, :, k : k + 1]
        turned = jnp.concatenate([-pivot[:, :, R:], pivot[:, :, :R]], axis=2)
        gain_r = jnp.where(row == k, 0.0, a[:, :, k : k + 1] * inverse)
        gain_i = jnp.where(row == k, 0.0, a[:, :, R + k : R + k + 1] * inverse)
        auto[...] = a - gain_r * pivot - gain_i * turned
        right_r = cross[:, k : k + 1, :]
        right_i = cross[:, R + k : R + k + 1, :]
        cross[:, :R, :] = cross[:, :R, :] - gain_r * right_r + gain_i * right_i
        cross[:, R:, :] = cross[:, R:, :] - gain_r * right_i - gain_i * right_r
    column = lax.broadcasted_iota(jnp.int32, (1, R, 2 * R), 2)
    diagonal = jnp.sum(jnp.where(column == lax.broadcasted_iota(jnp.int32, (1, R, 2 * R), 1), auto[...], 0.0), axis=2, keepdims=True)
    scale = 1.0 / diagonal
    out_ref[:, 0] = cross[:, :R, :] * scale
    out_ref[:, 1] = cross[:, R:, :] * scale


def solve(lines, refs):
    return pl.pallas_call(
        solve_kernel,
        out_shape=jax.ShapeDtypeStruct((LN, 2, R, CL), jnp.float32),
        in_specs=[pl.BlockSpec(memory_space=pltpu.VMEM)] * 2,
        out_specs=pl.BlockSpec(memory_space=pltpu.VMEM),
        scratch_shapes=[pltpu.VMEM((LN, R, 2 * R), jnp.float32), pltpu.VMEM((LN, 2 * R, CL), jnp.float32)],
        compiler_params=pltpu.CompilerParams(vmem_limit_bytes=48 * 1024 * 1024),
    )(lines, refs)


def local(ref_signals, responses):
    sent = transform(dft_table(), responses, ref_signals.reshape(RL * S, L))
    lines = lax.all_to_all(sent, "seg", 0, 0, tiled=True)
    refs = lax.all_gather(lines[:, LN * ROWS : LN * ROWS + S, :].reshape(NSEG * S, 128), "chan")
    return solve(lines, refs)


def solution(mesh):
    placed = (P("chan", "seg"), P("chan", "seg"))
    return jax.shard_map(
        local, mesh=mesh, in_specs=placed, out_specs=P("seg", None, None, "chan"), check_vma=False
    )
```

```python
import jax
import jax.numpy as jnp
import numpy as np
from jax import lax
from jax.experimental import pallas as pl
from jax.experimental.pallas import tpu as pltpu
from jax.sharding import PartitionSpec as P

L = 2048
FB = 512
NSEG = 32
NCHAN = 8
S = 8
LN = FB // NSEG
R = 32
RL = R // NCHAN
CL = 128
ROWS = 2 * S
DEPTH = NSEG * ROWS
VMEM_LIMIT = 60 * 1024 * 1024


def dft_table():
    n = np.arange(L, dtype=np.int64)[None, :]
    k = np.arange(FB, dtype=np.int64)[:, None]
    phase = (n * k % L) * (2.0 * np.pi / L)
    window = 0.5 - 0.5 * np.cos(n * (2.0 * np.pi / L))
    table = np.stack([window * np.cos(phase), -window * np.sin(phase)], axis=1)
    return jnp.asarray(table.reshape(2 * FB, L), dtype=jnp.bfloat16)


def whole():
    return pl.BlockSpec(memory_space=pltpu.VMEM)


def cost(flops, nbytes):
    return pl.CostEstimate(flops=flops, bytes_accessed=nbytes, transcendentals=0)


def params():
    return pltpu.CompilerParams(vmem_limit_bytes=VMEM_LIMIT)


def away():
    return pl.BlockSpec(memory_space=pl.ANY)


def fetch(pairs, sems):
    copies = [pltpu.make_async_copy(src, dst, sems.at[i]) for i, (src, dst) in enumerate(pairs)]
    for copy in copies:
        copy.start()
    return copies


def transform_kernel(table_hbm, resp_hbm, out_hbm, table, resp, mixed, out, sems, out_sems):
    cuts, pairs = 4, S // 2
    rows, some = 2 * FB // cuts, NSEG // cuts
    wanted = [(resp_hbm.at[:, pl.ds(0, 2 * L)], resp.at[0])]
    wanted += [(table_hbm.at[pl.ds(q * rows, rows)], table.at[pl.ds(q * rows, rows)]) for q in range(cuts)]
    wanted += [(resp_hbm.at[:, pl.ds(2 * p * L, 2 * L)], resp.at[p]) for p in range(1, pairs)]
    copies = fetch(wanted, sems)
    sent = []
    for p in range(pairs):
        copies[p + cuts if p else 0].wait()
        pair = jnp.concatenate([resp[p, :, :L], resp[p, :, L:]], axis=0)
        for q in range(cuts):
            if p == 0:
                copies[1 + q].wait()
            lines = lax.dot_general(
                table[q * rows : (q + 1) * rows, :], pair, (((1,), (1,)), ((), ())), preferred_element_type=jnp.float32
            )
            for i in range(2):
                mixed[pl.ds(q * rows * S + 2 * p + i, rows, stride=S), :] = lines[:, i * CL : (i + 1) * CL]
            if p == pairs - 1:
                for d in range(q * some, (q + 1) * some):
                    out[d] = mixed[d * LN * ROWS : (d + 1) * LN * ROWS, :].astype(jnp.bfloat16)
                part = pl.ds(q * some, some)
                sent.append(pltpu.make_async_copy(out.at[part], out_hbm.at[part], out_sems.at[q]))
                sent[-1].start()
    for copy in sent:
        copy.wait()


def transform(table, responses):
    out = (NSEG, LN * ROWS, CL)
    return pl.pallas_call(
        transform_kernel,
        in_specs=[away(), away()],
        out_specs=away(),
        out_shape=jax.ShapeDtypeStruct(out, jnp.bfloat16),
        scratch_shapes=[
            pltpu.VMEM((2 * FB, L), jnp.bfloat16),
            pltpu.VMEM((S // 2, CL, 2 * L), jnp.bfloat16),
            pltpu.VMEM((2 * FB * S, CL), jnp.float32),
            pltpu.VMEM(out, jnp.bfloat16),
            pltpu.SemaphoreType.DMA((8,)),
            pltpu.SemaphoreType.DMA((4,)),
        ],
        compiler_params=params(),
        cost_estimate=cost(2 * 2 * FB * L * CL * S, 12_000_000),
    )(table, responses)


def ref_kernel(table_hbm, ref_ref, out_ref, table, sems):
    cuts = 4
    rows, some = 2 * FB // cuts, NSEG // cuts
    copies = fetch([(table_hbm.at[pl.ds(q * rows, rows)], table.at[pl.ds(q * rows, rows)]) for q in range(cuts)], sems)
    x = ref_ref[...].astype(jnp.float32)
    x = jnp.concatenate([x[r : r + 1, s * L : (s + 1) * L] for r in range(RL) for s in range(S)], axis=0)
    x = x.astype(jnp.bfloat16)
    w = LN * 2
    for q in range(cuts):
        copies[q].wait()
        spec = lax.dot_general(
            x, table[q * rows : (q + 1) * rows, :], (((1,), (1,)), ((), ())), preferred_element_type=jnp.float32
        )
        for d in range(some):
            tile = jnp.concatenate([spec[r * S : (r + 1) * S, d * w : (d + 1) * w] for r in range(RL)], axis=1)
            out_ref[q * some + d] = jnp.concatenate([tile, jnp.zeros_like(tile)], axis=0).astype(jnp.bfloat16)


def ref_transform(table, refs):
    return pl.pallas_call(
        ref_kernel,
        in_specs=[away(), whole()],
        out_specs=whole(),
        out_shape=jax.ShapeDtypeStruct((NSEG, ROWS, 128), jnp.bfloat16),
        scratch_shapes=[pltpu.VMEM((2 * FB, L), jnp.bfloat16), pltpu.SemaphoreType.DMA((4,))],
        compiler_params=params(),
        cost_estimate=cost(2 * 2 * FB * L * RL * S, 5_000_000),
    )(table, refs)


def spots(shape, target):
    row = lax.broadcasted_iota(jnp.int32, shape, 0)
    column = lax.broadcasted_iota(jnp.int32, shape, 1)
    return jnp.where(column == target(row), 1.0, 0.0).astype(jnp.bfloat16)


def exact(left, right, dims):
    return lax.dot_general(left, right, (dims, ((), ())), preferred_element_type=jnp.float32).astype(jnp.bfloat16)


def three(a):
    parts = []
    for _ in range(3):
        parts.append(a.astype(jnp.bfloat16))
        a = a - parts[-1].astype(jnp.float32)
    return parts


def invert_kernel(ref_ref, out_ref, left, state):
    wide = jnp.concatenate([ref_ref[c] for c in range(NCHAN)], axis=1)
    halves = []
    for part in range(2):
        pick = spots(
            (LN * R, NCHAN * 128),
            lambda i: (i // RL) % NCHAN * 128 + i % RL * (2 * LN) + i // R * 2 + part,
        )
        halves.append(exact(pick, wide, ((1,), (1,))))
    real, imag = halves
    put = [spots((NSEG * S, DEPTH), lambda i: i // S * ROWS + part * S + i % S) for part in range(2)]
    inner = ((1,), (0,))
    upper = exact(real, put[0], inner) + exact(imag, put[1], inner)
    lower = exact(real, put[1], inner) - exact(imag, put[0], inner)
    row = lax.broadcasted_iota(jnp.int32, (R, R), 0)
    column = lax.broadcasted_iota(jnp.int32, (R, R), 1)
    unit = jnp.where(row == column, 1.0, 0.0)
    for k in range(LN):
        rows = slice(k * R, (k + 1) * R)
        both = jnp.concatenate([upper[rows], lower[rows]], axis=0)
        left[k] = both
        own = lax.dot_general(both, upper[rows], (((1,), (1,)), ((), ())), preferred_element_type=jnp.float32)
        state[k] = jnp.concatenate([own[:R], own[R:], unit, jnp.zeros_like(unit)], axis=1)
    row = lax.broadcasted_iota(jnp.int32, (1, R, 1), 1)
    for k in range(R):
        a = state[...]
        pivot = state[:, k : k + 1, :]
        scale = 1.0 / pivot[:, :, k : k + 1]
        turned = jnp.concatenate(
            [-pivot[:, :, R : 2 * R], pivot[:, :, :R], -pivot[:, :, 3 * R :], pivot[:, :, 2 * R : 3 * R]], axis=2
        )
        gain_r = jnp.where(row == k, 0.0, a[:, :, k : k + 1] * scale)
        gain_i = jnp.where(row == k, 0.0, a[:, :, R + k : R + k + 1] * scale)
        state[...] = a - gain_r * pivot - gain_i * turned
    a = state[...]
    row = lax.broadcasted_iota(jnp.int32, (1, R, 4 * R), 1)
    column = lax.broadcasted_iota(jnp.int32, (1, R, 4 * R), 2)
    a = a * (1.0 / jnp.sum(jnp.where(column == row, a, 0.0), axis=2, keepdims=True))
    inv_r, inv_i = a[:, :, 2 * R : 3 * R], a[:, :, 3 * R :]
    for k in range(LN):
        inverse = jnp.concatenate(
            [
                jnp.concatenate([inv_r[k], -inv_i[k]], axis=1),
                jnp.concatenate([inv_i[k], inv_r[k]], axis=1),
            ],
            axis=0,
        )
        terms = jnp.dot(jnp.concatenate(three(inverse), axis=0), left[k], preferred_element_type=jnp.float32)
        terms = terms[: 2 * R] + (terms[2 * R : 4 * R] + terms[4 * R :])
        out_ref[k] = jnp.concatenate(three(terms), axis=0)


def invert(refs):
    return pl.pallas_call(
        invert_kernel,
        out_shape=jax.ShapeDtypeStruct((LN, 6 * R, DEPTH), jnp.bfloat16),
        in_specs=[whole()],
        out_specs=whole(),
        scratch_shapes=[pltpu.VMEM((LN, 2 * R, DEPTH), jnp.bfloat16), pltpu.VMEM((LN, R, 4 * R), jnp.float32)],
        compiler_params=params(),
        cost_estimate=cost(6_000_000_000, 2_000_000),
    )(refs)


def apply_kernel(resp_hbm, left_hbm, out_hbm, resp, left, out, sems, out_sems):
    cuts = 4
    some = LN // cuts
    wanted = []
    for q in range(cuts):
        part, rows = pl.ds(q * some, some), pl.ds(q * some * ROWS, some * ROWS)
        wanted += [(left_hbm.at[part], left.at[part]), (resp_hbm.at[:, rows], resp.at[:, rows])]
    copies = fetch(wanted, sems)
    sent = []
    for q in range(cuts):
        copies[2 * q].wait()
        copies[2 * q + 1].wait()
        for k in range(q * some, (q + 1) * some):
            lines = resp[:, k * ROWS : (k + 1) * ROWS, :].reshape(DEPTH, CL)
            terms = jnp.dot(left[k], lines, preferred_element_type=jnp.float32)
            found = terms[: 2 * R] + (terms[2 * R : 4 * R] + terms[4 * R :])
            out[k, 0] = found[:R]
            out[k, 1] = found[R:]
        part = pl.ds(q * some, some)
        sent.append(pltpu.make_async_copy(out.at[part], out_hbm.at[part], out_sems.at[q]))
        sent[-1].start()
    for copy in sent:
        copy.wait()


def apply(lines, left):
    out = (LN, 2, R, CL)
    return pl.pallas_call(
        apply_kernel,
        out_shape=jax.ShapeDtypeStruct(out, jnp.float32),
        in_specs=[away(), away()],
        out_specs=away(),
        scratch_shapes=[
            pltpu.VMEM((NSEG, LN * ROWS, CL), jnp.bfloat16),
            pltpu.VMEM((LN, 6 * R, DEPTH), jnp.bfloat16),
            pltpu.VMEM(out, jnp.float32),
            pltpu.SemaphoreType.DMA((8,)),
            pltpu.SemaphoreType.DMA((4,)),
        ],
        compiler_params=params(),
        cost_estimate=cost(2_000_000_000, 4_000_000),
    )(lines, left)


def local(ref_signals, responses):
    table = dft_table()
    tiles = ref_transform(table, ref_signals)
    tiles, responses = lax.optimization_barrier((tiles, responses))
    tiles = lax.all_to_all(tiles, "seg", 0, 0, tiled=True)
    lines = lax.all_to_all(transform(table, responses), "seg", 0, 0, tiled=True)
    refs = lax.all_gather(tiles[:, :S, :].reshape(NSEG * S, 128), "chan")
    return apply(lines, invert(refs))


def solution(mesh):
    placed = (P("chan", "seg"), P("chan", "seg"))
    return jax.shard_map(
        local, mesh=mesh, in_specs=placed, out_specs=P("seg", None, None, "chan"), check_vma=False
    )
```

```python
import jax
import jax.numpy as jnp
import numpy as np
from jax import lax
from jax.experimental import pallas as pl
from jax.experimental.pallas import tpu as pltpu
from jax.sharding import PartitionSpec as P

L = 2048
FB = 512
NSEG = 32
NCHAN = 8
S = 8
LN = FB // NSEG
R = 32
RL = R // NCHAN
CL = 128
ROWS = 2 * S
DEPTH = NSEG * ROWS
NY, NZ = 4, 8


def dft_table():
    n = np.arange(L, dtype=np.int64)[None, :]
    k = np.arange(FB, dtype=np.int64)[:, None]
    phase = (n * k % L) * (2.0 * np.pi / L)
    window = 0.5 - 0.5 * np.cos(n * (2.0 * np.pi / L))
    table = np.stack([window * np.cos(phase), -window * np.sin(phase)], axis=1)
    return jnp.asarray(table.reshape(2 * FB, L), dtype=jnp.bfloat16)


def whole():
    return pl.BlockSpec(memory_space=pltpu.VMEM)


def cost(flops, nbytes):
    return pl.CostEstimate(flops=flops, bytes_accessed=nbytes, transcendentals=0)


def params(mib=60):
    return pltpu.CompilerParams(vmem_limit_bytes=mib * 1024 * 1024)


def away():
    return pl.BlockSpec(memory_space=pl.ANY)


def fetch(pairs, sems):
    copies = [pltpu.make_async_copy(src, dst, sems.at[i]) for i, (src, dst) in enumerate(pairs)]
    for copy in copies:
        copy.start()
    return copies


def transform_kernel(table_hbm, resp_hbm, out_hbm, table, resp, mixed, out, sems, out_sems):
    cuts, pairs = 4, S // 2
    rows, some = 2 * FB // cuts, NSEG // cuts
    wanted = [(resp_hbm.at[:, pl.ds(0, 2 * L)], resp.at[0])]
    wanted += [(table_hbm.at[pl.ds(q * rows, rows)], table.at[pl.ds(q * rows, rows)]) for q in range(cuts)]
    wanted += [(resp_hbm.at[:, pl.ds(2 * p * L, 2 * L)], resp.at[p]) for p in range(1, pairs)]
    copies = fetch(wanted, sems)
    sent = []
    for p in range(pairs):
        copies[p + cuts if p else 0].wait()
        pair = jnp.concatenate([resp[p, :, :L], resp[p, :, L:]], axis=0)
        for q in range(cuts):
            if p == 0:
                copies[1 + q].wait()
            lines = lax.dot_general(
                table[q * rows : (q + 1) * rows, :], pair, (((1,), (1,)), ((), ())), preferred_element_type=jnp.float32
            )
            for i in range(2):
                mixed[pl.ds(q * rows * S + 2 * p + i, rows, stride=S), :] = lines[:, i * CL : (i + 1) * CL]
            if p == pairs - 1:
                for d in range(q * some, (q + 1) * some):
                    out[d] = mixed[d * LN * ROWS : (d + 1) * LN * ROWS, :].astype(jnp.bfloat16)
                part = pl.ds(q * some, some)
                sent.append(pltpu.make_async_copy(out.at[part], out_hbm.at[part], out_sems.at[q]))
                sent[-1].start()
    for copy in sent:
        copy.wait()


def transform(table, responses):
    out = (NSEG, LN * ROWS, CL)
    return pl.pallas_call(
        transform_kernel,
        in_specs=[away(), away()],
        out_specs=away(),
        out_shape=jax.ShapeDtypeStruct(out, jnp.bfloat16),
        scratch_shapes=[
            pltpu.VMEM((2 * FB, L), jnp.bfloat16),
            pltpu.VMEM((S // 2, CL, 2 * L), jnp.bfloat16),
            pltpu.VMEM((2 * FB * S, CL), jnp.float32),
            pltpu.VMEM(out, jnp.bfloat16),
            pltpu.SemaphoreType.DMA((8,)),
            pltpu.SemaphoreType.DMA((4,)),
        ],
        compiler_params=params(),
        cost_estimate=cost(2 * 2 * FB * L * CL * S, 12_000_000),
    )(table, responses)


def ref_kernel(table_hbm, ref_ref, out_ref, table, refs, sems):
    cuts = 2
    rows, some = 2 * FB // cuts, NSEG // cuts

    def piece(q):
        part = pl.ds(q * rows, rows)
        return pltpu.make_async_copy(table_hbm.at[part], table.at[part], sems.at[q])

    for q in range(cuts):
        piece(q).start()
    x = ref_ref[...].astype(jnp.float32)
    x = jnp.concatenate([x[r : r + 1, s * L : (s + 1) * L] for r in range(RL) for s in range(S)], axis=0)
    refs[...] = x.astype(jnp.bfloat16)
    w = LN * 2

    def body(q, carry):
        piece(q).wait()
        spec = lax.dot_general(
            refs[...], table[pl.ds(q * rows, rows), :], (((1,), (1,)), ((), ())), preferred_element_type=jnp.float32
        )
        for d in range(some):
            tile = jnp.concatenate([spec[r * S : (r + 1) * S, d * w : (d + 1) * w] for r in range(RL)], axis=1)
            tile = jnp.concatenate([tile, jnp.zeros_like(tile)], axis=0)
            out_ref[d % NZ, q * (some // NZ) + d // NZ] = tile.astype(jnp.bfloat16)
        return carry

    lax.fori_loop(0, cuts, body, 0)


def ref_transform(table, refs):
    return pl.pallas_call(
        ref_kernel,
        in_specs=[away(), whole()],
        out_specs=whole(),
        out_shape=jax.ShapeDtypeStruct((NZ, NY, ROWS, 128), jnp.bfloat16),
        scratch_shapes=[
            pltpu.VMEM((2 * FB, L), jnp.bfloat16),
            pltpu.VMEM((RL * S, L), jnp.bfloat16),
            pltpu.SemaphoreType.DMA((2,)),
        ],
        compiler_params=params(),
        cost_estimate=cost(2 * 2 * FB * L * RL * S, 5_000_000),
    )(table, refs)


def gather_refs(tiles):
    y = lax.axis_index("seg") // NZ
    got = []
    for dy in range(NY):
        slab = lax.dynamic_index_in_dim(tiles, (y + dy) % NY, 1, keepdims=False)
        if dy:
            slab = lax.ppermute(slab, "seg", [(i, (i + dy * NZ) % NSEG) for i in range(NSEG)])
        got.append(slab[:, :S])
    return lax.all_gather(jnp.stack(got).reshape(NSEG * S, 128), "chan")


def spots(shape, target):
    row = lax.broadcasted_iota(jnp.int32, shape, 0)
    column = lax.broadcasted_iota(jnp.int32, shape, 1)
    return jnp.where(column == target(row), 1.0, 0.0).astype(jnp.bfloat16)


def exact(left, right, dims):
    return lax.dot_general(left, right, (dims, ((), ())), preferred_element_type=jnp.float32).astype(jnp.bfloat16)


def three(a):
    parts = []
    for _ in range(3):
        parts.append(a.astype(jnp.bfloat16))
        a = a - parts[-1].astype(jnp.float32)
    return parts


def invert_kernel(y_ref, ref_ref, out_ref, left, state):
    y = y_ref[0]
    wide = jnp.concatenate([ref_ref[c] for c in range(NCHAN)], axis=1)
    halves = []
    for part in range(2):
        pick = spots(
            (LN * R, NCHAN * 128),
            lambda i: (i // RL) % NCHAN * 128 + i % RL * (2 * LN) + i // R * 2 + part,
        )
        halves.append(exact(pick, wide, ((1,), (1,))))
    real, imag = halves
    put = [spots((NSEG * S, DEPTH), lambda i: (((y - i // (NZ * S) + NY) % NY * NZ + i // S % NZ) * ROWS + part * S + i % S)) for part in range(2)]
    inner = ((1,), (0,))
    upper = exact(real, put[0], inner) + exact(imag, put[1], inner)
    lower = exact(real, put[1], inner) - exact(imag, put[0], inner)
    row = lax.broadcasted_iota(jnp.int32, (R, R), 0)
    column = lax.broadcasted_iota(jnp.int32, (R, R), 1)
    unit = jnp.where(row == column, 1.0, 0.0)
    for k in range(LN):
        rows = slice(k * R, (k + 1) * R)
        both = jnp.concatenate([upper[rows], lower[rows]], axis=0)
        left[k] = both
        own = lax.dot_general(both, upper[rows], (((1,), (1,)), ((), ())), preferred_element_type=jnp.float32)
        state[k] = jnp.concatenate([own[:R], own[R:], unit, jnp.zeros_like(unit)], axis=1)
    row = lax.broadcasted_iota(jnp.int32, (1, R, 1), 1)
    for k in range(R):
        a = state[...]
        pivot = state[:, k : k + 1, :]
        scale = 1.0 / pivot[:, :, k : k + 1]
        turned = jnp.concatenate(
            [-pivot[:, :, R : 2 * R], pivot[:, :, :R], -pivot[:, :, 3 * R :], pivot[:, :, 2 * R : 3 * R]], axis=2
        )
        gain_r = jnp.where(row == k, 0.0, a[:, :, k : k + 1] * scale)
        gain_i = jnp.where(row == k, 0.0, a[:, :, R + k : R + k + 1] * scale)
        state[...] = a - gain_r * pivot - gain_i * turned
    a = state[...]
    row = lax.broadcasted_iota(jnp.int32, (1, R, 4 * R), 1)
    column = lax.broadcasted_iota(jnp.int32, (1, R, 4 * R), 2)
    a = a * (1.0 / jnp.sum(jnp.where(column == row, a, 0.0), axis=2, keepdims=True))
    inv_r, inv_i = a[:, :, 2 * R : 3 * R], a[:, :, 3 * R :]
    for k in range(LN):
        inverse = jnp.concatenate(
            [
                jnp.concatenate([inv_r[k], -inv_i[k]], axis=1),
                jnp.concatenate([inv_i[k], inv_r[k]], axis=1),
            ],
            axis=0,
        )
        terms = jnp.dot(jnp.concatenate(three(inverse), axis=0), left[k], preferred_element_type=jnp.float32)
        terms = terms[: 2 * R] + (terms[2 * R : 4 * R] + terms[4 * R :])
        out_ref[k] = jnp.concatenate(three(terms), axis=0)


def invert(y, refs):
    return pl.pallas_call(
        invert_kernel,
        out_shape=jax.ShapeDtypeStruct((LN, 6 * R, DEPTH), jnp.bfloat16),
        in_specs=[pl.BlockSpec(memory_space=pltpu.SMEM), whole()],
        out_specs=whole(),
        scratch_shapes=[pltpu.VMEM((LN, 2 * R, DEPTH), jnp.bfloat16), pltpu.VMEM((LN, R, 4 * R), jnp.float32)],
        compiler_params=params(),
        cost_estimate=cost(6_000_000_000, 2_000_000),
    )(y, refs)


def apply_kernel(resp_ref, left_ref, out_ref):
    for k in range(LN):
        lines = resp_ref[:, k * ROWS : (k + 1) * ROWS, :].reshape(DEPTH, CL)
        terms = jnp.dot(left_ref[k], lines, preferred_element_type=jnp.float32)
        found = terms[: 2 * R] + (terms[2 * R : 4 * R] + terms[4 * R :])
        out_ref[k, 0] = found[:R]
        out_ref[k, 1] = found[R:]


def apply(lines, left):
    return pl.pallas_call(
        apply_kernel,
        out_shape=jax.ShapeDtypeStruct((LN, 2, R, CL), jnp.float32),
        in_specs=[whole(), whole()],
        out_specs=whole(),
        compiler_params=params(12),
        cost_estimate=cost(2_000_000_000, 4_000_000),
    )(lines, left)


def local(ref_signals, responses):
    table = dft_table()
    tiles = ref_transform(table, ref_signals)
    tiles, responses = lax.optimization_barrier((tiles, responses))
    along_z = [[y * NZ + z for z in range(NZ)] for y in range(NY)]
    tiles = lax.all_to_all(tiles, "seg", 0, 0, axis_index_groups=along_z, tiled=True)
    sent = transform(table, responses)
    sent, tiles = lax.optimization_barrier((sent, tiles))
    lines = lax.all_to_all(sent, "seg", 0, 0, tiled=True)
    y = (lax.axis_index("seg") // NZ).astype(jnp.int32).reshape(1)
    return apply(lines, invert(y, gather_refs(tiles)))


def solution(mesh):
    placed = (P("chan", "seg"), P("chan", "seg"))
    return jax.shard_map(
        local, mesh=mesh, in_specs=placed, out_specs=P("seg", None, None, "chan"), check_vma=False
    )
```

```python
import jax
import jax.numpy as jnp
import numpy as np
from jax import lax
from jax.experimental import pallas as pl
from jax.experimental.pallas import tpu as pltpu
from jax.sharding import PartitionSpec as P

L = 2048
FB = 512
NSEG = 32
NCHAN = 8
S = 8
LN = FB // NSEG
R = 32
RL = R // NCHAN
CL = 128
ROWS = 2 * S
DEPTH = NSEG * ROWS
NY, NZ = 4, 8


def dft_table():
    n = np.arange(L, dtype=np.int64)[None, :]
    k = np.arange(FB, dtype=np.int64)[:, None]
    phase = (n * k % L) * (2.0 * np.pi / L)
    window = 0.5 - 0.5 * np.cos(n * (2.0 * np.pi / L))
    table = np.stack([window * np.cos(phase), -window * np.sin(phase)], axis=1)
    return jnp.asarray(table.reshape(2 * FB, L), dtype=jnp.bfloat16)


def whole():
    return pl.BlockSpec(memory_space=pltpu.VMEM)


def cost(flops, nbytes):
    return pl.CostEstimate(flops=flops, bytes_accessed=nbytes, transcendentals=0)


def params(mib=60):
    return pltpu.CompilerParams(vmem_limit_bytes=mib * 1024 * 1024)


def away():
    return pl.BlockSpec(memory_space=pl.ANY)


def fetch(pairs, sems):
    copies = [pltpu.make_async_copy(src, dst, sems.at[i]) for i, (src, dst) in enumerate(pairs)]
    for copy in copies:
        copy.start()
    return copies


def transform_kernel(table_hbm, resp_hbm, out_hbm, table, resp, mixed, out, sems, out_sems):
    cuts, pairs = 4, S // 2
    rows, some = 2 * FB // cuts, NSEG // cuts
    wanted = [(resp_hbm.at[:, pl.ds(0, 2 * L)], resp.at[0])]
    wanted += [(table_hbm.at[pl.ds(q * rows, rows)], table.at[pl.ds(q * rows, rows)]) for q in range(cuts)]
    wanted += [(resp_hbm.at[:, pl.ds(2 * p * L, 2 * L)], resp.at[p]) for p in range(1, pairs)]
    copies = fetch(wanted, sems)
    for copy in copies[: 1 + cuts]:
        copy.wait()
    sent = []
    for p in range(pairs):
        if p:
            copies[p + cuts].wait()
        pair = jnp.concatenate([resp[p, :, :L], resp[p, :, L:]], axis=0)
        for q in range(cuts):
            lines = lax.dot_general(
                table[q * rows : (q + 1) * rows, :], pair, (((1,), (1,)), ((), ())), preferred_element_type=jnp.float32
            )
            for i in range(2):
                mixed[pl.ds(q * rows * S + 2 * p + i, rows, stride=S), :] = lines[:, i * CL : (i + 1) * CL]
            if p == pairs - 1:
                for d in range(q * some, (q + 1) * some):
                    out[d] = mixed[d * LN * ROWS : (d + 1) * LN * ROWS, :].astype(jnp.bfloat16)
                part = pl.ds(q * some, some)
                sent.append(pltpu.make_async_copy(out.at[part], out_hbm.at[part], out_sems.at[q]))
                sent[-1].start()
    for copy in sent:
        copy.wait()


def transform(table, responses):
    out = (NSEG, LN * ROWS, CL)
    return pl.pallas_call(
        transform_kernel,
        in_specs=[away(), away()],
        out_specs=away(),
        out_shape=jax.ShapeDtypeStruct(out, jnp.bfloat16),
        scratch_shapes=[
            pltpu.VMEM((2 * FB, L), jnp.bfloat16),
            pltpu.VMEM((S // 2, CL, 2 * L), jnp.bfloat16),
            pltpu.VMEM((2 * FB * S, CL), jnp.float32),
            pltpu.VMEM(out, jnp.bfloat16),
            pltpu.SemaphoreType.DMA((8,)),
            pltpu.SemaphoreType.DMA((4,)),
        ],
        compiler_params=params(),
        cost_estimate=cost(2 * 2 * FB * L * CL * S, 12_000_000),
    )(table, responses)


def ref_kernel(table_hbm, ref_ref, out_ref, table, refs, sems):
    cuts = 2
    rows, some = 2 * FB // cuts, NSEG // cuts

    def piece(q):
        part = pl.ds(q * rows, rows)
        return pltpu.make_async_copy(table_hbm.at[part], table.at[part], sems.at[q])

    for q in range(cuts):
        piece(q).start()
    x = ref_ref[...].astype(jnp.float32)
    x = jnp.concatenate([x[r : r + 1, s * L : (s + 1) * L] for r in range(RL) for s in range(S)], axis=0)
    refs[...] = x.astype(jnp.bfloat16)
    w = LN * 2

    def body(q, carry):
        piece(q).wait()
        spec = lax.dot_general(
            refs[...], table[pl.ds(q * rows, rows), :], (((1,), (1,)), ((), ())), preferred_element_type=jnp.float32
        )
        for d in range(some):
            tile = jnp.concatenate([spec[r * S : (r + 1) * S, d * w : (d + 1) * w] for r in range(RL)], axis=1)
            tile = jnp.concatenate([tile, jnp.zeros_like(tile)], axis=0)
            out_ref[d % NZ, q * (some // NZ) + d // NZ] = tile.astype(jnp.bfloat16)
        return carry

    lax.fori_loop(0, cuts, body, 0)


def ref_transform(table, refs):
    return pl.pallas_call(
        ref_kernel,
        in_specs=[away(), whole()],
        out_specs=whole(),
        out_shape=jax.ShapeDtypeStruct((NZ, NY, ROWS, 128), jnp.bfloat16),
        scratch_shapes=[
            pltpu.VMEM((2 * FB, L), jnp.bfloat16),
            pltpu.VMEM((RL * S, L), jnp.bfloat16),
            pltpu.SemaphoreType.DMA((2,)),
        ],
        compiler_params=params(),
        cost_estimate=cost(2 * 2 * FB * L * RL * S, 5_000_000),
    )(table, refs)


def gather_refs(tiles):
    y = lax.axis_index("seg") // NZ
    got = []
    for dy in range(NY):
        slab = lax.dynamic_index_in_dim(tiles, (y + dy) % NY, 1, keepdims=False)
        if dy:
            slab = lax.ppermute(slab, "seg", [(i, (i + dy * NZ) % NSEG) for i in range(NSEG)])
        got.append(slab[:, :S])
    return lax.all_gather(jnp.stack(got).reshape(NSEG * S, 128), "chan")


def spots(shape, target):
    row = lax.broadcasted_iota(jnp.int32, shape, 0)
    column = lax.broadcasted_iota(jnp.int32, shape, 1)
    return jnp.where(column == target(row), 1.0, 0.0).astype(jnp.bfloat16)


def exact(left, right, dims):
    return lax.dot_general(left, right, (dims, ((), ())), preferred_element_type=jnp.float32).astype(jnp.bfloat16)


def three(a):
    parts = []
    for _ in range(3):
        parts.append(a.astype(jnp.bfloat16))
        a = a - parts[-1].astype(jnp.float32)
    return parts


def invert_kernel(y_ref, ref_ref, out_ref, left, state):
    y = y_ref[0]
    wide = jnp.concatenate([ref_ref[c] for c in range(NCHAN)], axis=1)
    halves = []
    for part in range(2):
        pick = spots(
            (LN * R, NCHAN * 128),
            lambda i: (i // RL) % NCHAN * 128 + i % RL * (2 * LN) + i // R * 2 + part,
        )
        halves.append(exact(pick, wide, ((1,), (1,))))
    real, imag = halves
    put = [spots((NSEG * S, DEPTH), lambda i: (((y - i // (NZ * S) + NY) % NY * NZ + i // S % NZ) * ROWS + part * S + i % S)) for part in range(2)]
    inner = ((1,), (0,))
    upper = exact(real, put[0], inner) + exact(imag, put[1], inner)
    lower = exact(real, put[1], inner) - exact(imag, put[0], inner)
    row = lax.broadcasted_iota(jnp.int32, (R, R), 0)
    column = lax.broadcasted_iota(jnp.int32, (R, R), 1)
    unit = jnp.where(row == column, 1.0, 0.0)
    for k in range(LN):
        rows = slice(k * R, (k + 1) * R)
        both = jnp.concatenate([upper[rows], lower[rows]], axis=0)
        left[k] = both
        own = lax.dot_general(both, upper[rows], (((1,), (1,)), ((), ())), preferred_element_type=jnp.float32)
        state[k] = jnp.concatenate([own[:R], own[R:], unit, jnp.zeros_like(unit)], axis=1)
    row = lax.broadcasted_iota(jnp.int32, (1, R, 1), 1)
    for k in range(R):
        a = state[...]
        pivot = state[:, k : k + 1, :]
        scale = 1.0 / pivot[:, :, k : k + 1]
        turned = jnp.concatenate(
            [-pivot[:, :, R : 2 * R], pivot[:, :, :R], -pivot[:, :, 3 * R :], pivot[:, :, 2 * R : 3 * R]], axis=2
        )
        gain_r = jnp.where(row == k, 0.0, a[:, :, k : k + 1] * scale)
        gain_i = jnp.where(row == k, 0.0, a[:, :, R + k : R + k + 1] * scale)
        state[...] = a - gain_r * pivot - gain_i * turned
    a = state[...]
    row = lax.broadcasted_iota(jnp.int32, (1, R, 4 * R), 1)
    column = lax.broadcasted_iota(jnp.int32, (1, R, 4 * R), 2)
    a = a * (1.0 / jnp.sum(jnp.where(column == row, a, 0.0), axis=2, keepdims=True))
    inv_r, inv_i = a[:, :, 2 * R : 3 * R], a[:, :, 3 * R :]
    for k in range(LN):
        inverse = jnp.concatenate(
            [
                jnp.concatenate([inv_r[k], -inv_i[k]], axis=1),
                jnp.concatenate([inv_i[k], inv_r[k]], axis=1),
            ],
            axis=0,
        )
        terms = jnp.dot(jnp.concatenate(three(inverse), axis=0), left[k], preferred_element_type=jnp.float32)
        terms = terms[: 2 * R] + (terms[2 * R : 4 * R] + terms[4 * R :])
        out_ref[k] = jnp.concatenate(three(terms), axis=0)


def invert(y, refs):
    return pl.pallas_call(
        invert_kernel,
        out_shape=jax.ShapeDtypeStruct((LN, 6 * R, DEPTH), jnp.bfloat16),
        in_specs=[pl.BlockSpec(memory_space=pltpu.SMEM), whole()],
        out_specs=whole(),
        scratch_shapes=[pltpu.VMEM((LN, 2 * R, DEPTH), jnp.bfloat16), pltpu.VMEM((LN, R, 4 * R), jnp.float32)],
        compiler_params=params(),
        cost_estimate=cost(6_000_000_000, 2_000_000),
    )(y, refs)


def apply_kernel(resp_ref, left_ref, out_ref):
    for k in range(LN):
        lines = resp_ref[:, k * ROWS : (k + 1) * ROWS, :].reshape(DEPTH, CL)
        terms = jnp.dot(left_ref[k], lines, preferred_element_type=jnp.float32)
        found = terms[: 2 * R] + (terms[2 * R : 4 * R] + terms[4 * R :])
        out_ref[k, 0] = found[:R]
        out_ref[k, 1] = found[R:]


def apply(lines, left):
    return pl.pallas_call(
        apply_kernel,
        out_shape=jax.ShapeDtypeStruct((LN, 2, R, CL), jnp.float32),
        in_specs=[whole(), whole()],
        out_specs=whole(),
        compiler_params=params(12),
        cost_estimate=cost(2_000_000_000, 4_000_000),
    )(lines, left)


def local(ref_signals, responses):
    table = dft_table()
    tiles = ref_transform(table, ref_signals)
    tiles, responses = lax.optimization_barrier((tiles, responses))
    along_z = [[y * NZ + z for z in range(NZ)] for y in range(NY)]
    tiles = lax.all_to_all(tiles, "seg", 0, 0, axis_index_groups=along_z, tiled=True)
    sent = transform(table, responses)
    sent, tiles = lax.optimization_barrier((sent, tiles))
    lines = lax.all_to_all(sent, "seg", 0, 0, tiled=True)
    y = (lax.axis_index("seg") // NZ).astype(jnp.int32).reshape(1)
    return apply(lines, invert(y, gather_refs(tiles)))


def solution(mesh):
    placed = (P("chan", "seg"), P("chan", "seg"))
    return jax.shard_map(
        local, mesh=mesh, in_specs=placed, out_specs=P("seg", None, None, "chan"), check_vma=False
    )
```

```python
import jax
import jax.numpy as jnp
import numpy as np
from jax import lax
from jax.experimental import pallas as pl
from jax.experimental.pallas import tpu as pltpu
from jax.sharding import PartitionSpec as P

L = 2048
FB = 512
NSEG = 32
NCHAN = 8
S = 8
LN = FB // NSEG
R = 32
RL = R // NCHAN
CL = 128
ROWS = 2 * S
DEPTH = NSEG * ROWS
NY, NZ = 4, 8


def dft_table():
    n = np.arange(L, dtype=np.int64)[None, :]
    k = np.arange(FB, dtype=np.int64)[:, None]
    phase = (n * k % L) * (2.0 * np.pi / L)
    window = 0.5 - 0.5 * np.cos(n * (2.0 * np.pi / L))
    table = np.stack([window * np.cos(phase), -window * np.sin(phase)], axis=1)
    return jnp.asarray(table.reshape(2 * FB, L), dtype=jnp.bfloat16)


def whole():
    return pl.BlockSpec(memory_space=pltpu.VMEM)


def cost(flops, nbytes):
    return pl.CostEstimate(flops=flops, bytes_accessed=nbytes, transcendentals=0)


def params(mib=60):
    return pltpu.CompilerParams(vmem_limit_bytes=mib * 1024 * 1024)


def away():
    return pl.BlockSpec(memory_space=pl.ANY)


def fetch(pairs, sems):
    copies = [pltpu.make_async_copy(src, dst, sems.at[i]) for i, (src, dst) in enumerate(pairs)]
    for copy in copies:
        copy.start()
    return copies


def transform_kernel(table_hbm, resp_hbm, out_hbm, table, resp, mixed, out, sems, out_sems):
    cuts, pairs = 4, S // 2
    rows, some = 2 * FB // cuts, NSEG // cuts
    wanted = [(resp_hbm.at[:, pl.ds(0, 2 * L)], resp.at[0])]
    wanted += [(table_hbm.at[pl.ds(q * rows, rows)], table.at[pl.ds(q * rows, rows)]) for q in range(cuts)]
    wanted += [(resp_hbm.at[:, pl.ds(2 * p * L, 2 * L)], resp.at[p]) for p in range(1, pairs)]
    copies = fetch(wanted, sems)
    for copy in copies[: 1 + cuts]:
        copy.wait()
    sent = []
    for p in range(pairs):
        if p == 1:
            for copy in copies[1 + cuts :]:
                copy.wait()
        pair = jnp.concatenate([resp[p, :, :L], resp[p, :, L:]], axis=0)
        for q in range(cuts):
            lines = lax.dot_general(
                table[q * rows : (q + 1) * rows, :], pair, (((1,), (1,)), ((), ())), preferred_element_type=jnp.float32
            )
            for i in range(2):
                mixed[pl.ds(q * rows * S + 2 * p + i, rows, stride=S), :] = lines[:, i * CL : (i + 1) * CL]
            if p == pairs - 1:
                for d in range(q * some, (q + 1) * some):
                    out[d] = mixed[d * LN * ROWS : (d + 1) * LN * ROWS, :].astype(jnp.bfloat16)
                part = pl.ds(q * some, some)
                sent.append(pltpu.make_async_copy(out.at[part], out_hbm.at[part], out_sems.at[q]))
                sent[-1].start()
    for copy in sent:
        copy.wait()


def transform(table, responses):
    out = (NSEG, LN * ROWS, CL)
    return pl.pallas_call(
        transform_kernel,
        in_specs=[away(), away()],
        out_specs=away(),
        out_shape=jax.ShapeDtypeStruct(out, jnp.bfloat16),
        scratch_shapes=[
            pltpu.VMEM((2 * FB, L), jnp.bfloat16),
            pltpu.VMEM((S // 2, CL, 2 * L), jnp.bfloat16),
            pltpu.VMEM((2 * FB * S, CL), jnp.float32),
            pltpu.VMEM(out, jnp.bfloat16),
            pltpu.SemaphoreType.DMA((8,)),
            pltpu.SemaphoreType.DMA((4,)),
        ],
        compiler_params=params(),
        cost_estimate=cost(2 * 2 * FB * L * CL * S, 12_000_000),
    )(table, responses)


def ref_kernel(table_hbm, ref_ref, out_ref, table, refs, sems):
    cuts = 2
    rows, some = 2 * FB // cuts, NSEG // cuts

    def piece(q):
        part = pl.ds(q * rows, rows)
        return pltpu.make_async_copy(table_hbm.at[part], table.at[part], sems.at[q])

    for q in range(cuts):
        piece(q).start()
    x = ref_ref[...].astype(jnp.float32)
    x = jnp.concatenate([x[r : r + 1, s * L : (s + 1) * L] for r in range(RL) for s in range(S)], axis=0)
    refs[...] = x.astype(jnp.bfloat16)
    w = LN * 2

    def body(q, carry):
        piece(q).wait()
        spec = lax.dot_general(
            refs[...], table[pl.ds(q * rows, rows), :], (((1,), (1,)), ((), ())), preferred_element_type=jnp.float32
        )
        for d in range(some):
            tile = jnp.concatenate([spec[r * S : (r + 1) * S, d * w : (d + 1) * w] for r in range(RL)], axis=1)
            tile = jnp.concatenate([tile, jnp.zeros_like(tile)], axis=0)
            out_ref[d % NZ, q * (some // NZ) + d // NZ] = tile.astype(jnp.bfloat16)
        return carry

    lax.fori_loop(0, cuts, body, 0)


def ref_transform(table, refs):
    return pl.pallas_call(
        ref_kernel,
        in_specs=[away(), whole()],
        out_specs=whole(),
        out_shape=jax.ShapeDtypeStruct((NZ, NY, ROWS, 128), jnp.bfloat16),
        scratch_shapes=[
            pltpu.VMEM((2 * FB, L), jnp.bfloat16),
            pltpu.VMEM((RL * S, L), jnp.bfloat16),
            pltpu.SemaphoreType.DMA((2,)),
        ],
        compiler_params=params(),
        cost_estimate=cost(2 * 2 * FB * L * RL * S, 5_000_000),
    )(table, refs)


def gather_refs(tiles):
    y = lax.axis_index("seg") // NZ
    got = []
    for dy in range(NY):
        slab = lax.dynamic_index_in_dim(tiles, (y + dy) % NY, 1, keepdims=False)
        if dy:
            slab = lax.ppermute(slab, "seg", [(i, (i + dy * NZ) % NSEG) for i in range(NSEG)])
        got.append(slab[:, :S])
    return lax.all_gather(jnp.stack(got).reshape(NSEG * S, 128), "chan")


def spots(shape, target):
    row = lax.broadcasted_iota(jnp.int32, shape, 0)
    column = lax.broadcasted_iota(jnp.int32, shape, 1)
    return jnp.where(column == target(row), 1.0, 0.0).astype(jnp.bfloat16)


def exact(left, right, dims):
    return lax.dot_general(left, right, (dims, ((), ())), preferred_element_type=jnp.float32).astype(jnp.bfloat16)


def three(a):
    parts = []
    for _ in range(3):
        parts.append(a.astype(jnp.bfloat16))
        a = a - parts[-1].astype(jnp.float32)
    return parts


def invert_kernel(y_ref, ref_ref, out_ref, left, state):
    y = y_ref[0]
    wide = jnp.concatenate([ref_ref[c] for c in range(NCHAN)], axis=1)
    halves = []
    for part in range(2):
        pick = spots(
            (LN * R, NCHAN * 128),
            lambda i: (i // RL) % NCHAN * 128 + i % RL * (2 * LN) + i // R * 2 + part,
        )
        halves.append(exact(pick, wide, ((1,), (1,))))
    real, imag = halves
    put = [spots((NSEG * S, DEPTH), lambda i: (((y - i // (NZ * S) + NY) % NY * NZ + i // S % NZ) * ROWS + part * S + i % S)) for part in range(2)]
    inner = ((1,), (0,))
    upper = exact(real, put[0], inner) + exact(imag, put[1], inner)
    lower = exact(real, put[1], inner) - exact(imag, put[0], inner)
    row = lax.broadcasted_iota(jnp.int32, (R, R), 0)
    column = lax.broadcasted_iota(jnp.int32, (R, R), 1)
    unit = jnp.where(row == column, 1.0, 0.0)
    for k in range(LN):
        rows = slice(k * R, (k + 1) * R)
        both = jnp.concatenate([upper[rows], lower[rows]], axis=0)
        left[k] = both
        own = lax.dot_general(both, upper[rows], (((1,), (1,)), ((), ())), preferred_element_type=jnp.float32)
        state[k] = jnp.concatenate([own[:R], own[R:], unit, jnp.zeros_like(unit)], axis=1)
    row = lax.broadcasted_iota(jnp.int32, (1, R, 1), 1)
    for k in range(R):
        a = state[...]
        pivot = state[:, k : k + 1, :]
        scale = 1.0 / pivot[:, :, k : k + 1]
        turned = jnp.concatenate(
            [-pivot[:, :, R : 2 * R], pivot[:, :, :R], -pivot[:, :, 3 * R :], pivot[:, :, 2 * R : 3 * R]], axis=2
        )
        gain_r = jnp.where(row == k, 0.0, a[:, :, k : k + 1] * scale)
        gain_i = jnp.where(row == k, 0.0, a[:, :, R + k : R + k + 1] * scale)
        state[...] = a - gain_r * pivot - gain_i * turned
    a = state[...]
    row = lax.broadcasted_iota(jnp.int32, (1, R, 4 * R), 1)
    column = lax.broadcasted_iota(jnp.int32, (1, R, 4 * R), 2)
    a = a * (1.0 / jnp.sum(jnp.where(column == row, a, 0.0), axis=2, keepdims=True))
    inv_r, inv_i = a[:, :, 2 * R : 3 * R], a[:, :, 3 * R :]
    for k in range(LN):
        inverse = jnp.concatenate(
            [
                jnp.concatenate([inv_r[k], -inv_i[k]], axis=1),
                jnp.concatenate([inv_i[k], inv_r[k]], axis=1),
            ],
            axis=0,
        )
        terms = jnp.dot(jnp.concatenate(three(inverse), axis=0), left[k], preferred_element_type=jnp.float32)
        terms = terms[: 2 * R] + (terms[2 * R : 4 * R] + terms[4 * R :])
        out_ref[k] = jnp.concatenate(three(terms), axis=0)


def invert(y, refs):
    return pl.pallas_call(
        invert_kernel,
        out_shape=jax.ShapeDtypeStruct((LN, 6 * R, DEPTH), jnp.bfloat16),
        in_specs=[pl.BlockSpec(memory_space=pltpu.SMEM), whole()],
        out_specs=whole(),
        scratch_shapes=[pltpu.VMEM((LN, 2 * R, DEPTH), jnp.bfloat16), pltpu.VMEM((LN, R, 4 * R), jnp.float32)],
        compiler_params=params(),
        cost_estimate=cost(6_000_000_000, 2_000_000),
    )(y, refs)


def apply_kernel(resp_ref, left_ref, out_ref):
    for k in range(LN):
        lines = resp_ref[:, k * ROWS : (k + 1) * ROWS, :].reshape(DEPTH, CL)
        terms = jnp.dot(left_ref[k], lines, preferred_element_type=jnp.float32)
        found = terms[: 2 * R] + (terms[2 * R : 4 * R] + terms[4 * R :])
        out_ref[k, 0] = found[:R]
        out_ref[k, 1] = found[R:]


def apply(lines, left):
    return pl.pallas_call(
        apply_kernel,
        out_shape=jax.ShapeDtypeStruct((LN, 2, R, CL), jnp.float32),
        in_specs=[whole(), whole()],
        out_specs=whole(),
        compiler_params=params(12),
        cost_estimate=cost(2_000_000_000, 4_000_000),
    )(lines, left)


def local(ref_signals, responses):
    table = dft_table()
    tiles = ref_transform(table, ref_signals)
    tiles, responses = lax.optimization_barrier((tiles, responses))
    along_z = [[y * NZ + z for z in range(NZ)] for y in range(NY)]
    tiles = lax.all_to_all(tiles, "seg", 0, 0, axis_index_groups=along_z, tiled=True)
    sent = transform(table, responses)
    sent, tiles = lax.optimization_barrier((sent, tiles))
    lines = lax.all_to_all(sent, "seg", 0, 0, tiled=True)
    y = (lax.axis_index("seg") // NZ).astype(jnp.int32).reshape(1)
    return apply(lines, invert(y, gather_refs(tiles)))


def solution(mesh):
    placed = (P("chan", "seg"), P("chan", "seg"))
    return jax.shard_map(
        local, mesh=mesh, in_specs=placed, out_specs=P("seg", None, None, "chan"), check_vma=False
    )
```

```python
import jax
import jax.numpy as jnp
import numpy as np
from jax import lax
from jax.experimental import pallas as pl
from jax.experimental.pallas import tpu as pltpu
from jax.sharding import PartitionSpec as P

L = 2048
FB = 512
NSEG = 32
NCHAN = 8
S = 8
LN = FB // NSEG
R = 32
RL = R // NCHAN
CL = 128
ROWS = 2 * S
DEPTH = NSEG * ROWS
NY, NZ = 4, 8


def dft_table():
    n = np.arange(L, dtype=np.int64)[None, :]
    k = np.arange(FB, dtype=np.int64)[:, None]
    phase = (n * k % L) * (2.0 * np.pi / L)
    window = 0.5 - 0.5 * np.cos(n * (2.0 * np.pi / L))
    table = np.stack([window * np.cos(phase), -window * np.sin(phase)], axis=1)
    return jnp.asarray(table.reshape(2 * FB, L), dtype=jnp.bfloat16)


def whole():
    return pl.BlockSpec(memory_space=pltpu.VMEM)


def cost(flops, nbytes):
    return pl.CostEstimate(flops=flops, bytes_accessed=nbytes, transcendentals=0)


def params(mib=60):
    return pltpu.CompilerParams(vmem_limit_bytes=mib * 1024 * 1024)


def away():
    return pl.BlockSpec(memory_space=pl.ANY)


def fetch(pairs, sems):
    copies = [pltpu.make_async_copy(src, dst, sems.at[i]) for i, (src, dst) in enumerate(pairs)]
    for copy in copies:
        copy.start()
    return copies


def transform_kernel(table_hbm, resp_hbm, out_hbm, table, resp, mixed, out, sems, out_sems):
    cuts, pairs = 4, S // 2
    rows, some = 2 * FB // cuts, NSEG // cuts
    wanted = [(resp_hbm.at[:, pl.ds(0, 2 * L)], resp.at[0])]
    wanted += [(table_hbm.at[pl.ds(q * rows, rows)], table.at[pl.ds(q * rows, rows)]) for q in range(cuts)]
    wanted += [(resp_hbm.at[:, pl.ds(2 * p * L, 2 * L)], resp.at[p]) for p in range(1, pairs)]
    copies = fetch(wanted, sems)
    for copy in copies[: 1 + cuts]:
        copy.wait()
    sent = []
    for p in range(pairs):
        if p == 1:
            for copy in copies[1 + cuts :]:
                copy.wait()
        pair = jnp.concatenate([resp[p, :, :L], resp[p, :, L:]], axis=0)
        for q in range(cuts):
            lines = lax.dot_general(
                table[q * rows : (q + 1) * rows, :], pair, (((1,), (1,)), ((), ())), preferred_element_type=jnp.float32
            )
            for i in range(2):
                mixed[pl.ds(q * rows * S + 2 * p + i, rows, stride=S), :] = lines[:, i * CL : (i + 1) * CL]
            if p == pairs - 1:
                for d in range(q * some, (q + 1) * some):
                    out[d] = mixed[d * LN * ROWS : (d + 1) * LN * ROWS, :].astype(jnp.bfloat16)
                part = pl.ds(q * some, some)
                sent.append(pltpu.make_async_copy(out.at[part], out_hbm.at[part], out_sems.at[q]))
                sent[-1].start()
    for copy in sent:
        copy.wait()


def transform(table, responses):
    out = (NSEG, LN * ROWS, CL)
    return pl.pallas_call(
        transform_kernel,
        in_specs=[away(), away()],
        out_specs=away(),
        out_shape=jax.ShapeDtypeStruct(out, jnp.bfloat16),
        scratch_shapes=[
            pltpu.VMEM((2 * FB, L), jnp.bfloat16),
            pltpu.VMEM((S // 2, CL, 2 * L), jnp.bfloat16),
            pltpu.VMEM((2 * FB * S, CL), jnp.float32),
            pltpu.VMEM(out, jnp.bfloat16),
            pltpu.SemaphoreType.DMA((8,)),
            pltpu.SemaphoreType.DMA((4,)),
        ],
        compiler_params=params(),
        cost_estimate=cost(2 * 2 * FB * L * CL * S, 12_000_000),
    )(table, responses)


def ref_kernel(table_hbm, ref_ref, out_ref, table, refs, sems):
    cuts = 2
    rows, some = 2 * FB // cuts, NSEG // cuts

    def piece(q):
        part = pl.ds(q * rows, rows)
        return pltpu.make_async_copy(table_hbm.at[part], table.at[part], sems.at[q])

    for q in range(cuts):
        piece(q).start()
    x = ref_ref[...].astype(jnp.float32)
    x = jnp.concatenate([x[r : r + 1, s * L : (s + 1) * L] for r in range(RL) for s in range(S)], axis=0)
    refs[...] = x.astype(jnp.bfloat16)
    w = LN * 2

    def body(q, carry):
        piece(q).wait()
        spec = lax.dot_general(
            refs[...], table[pl.ds(q * rows, rows), :], (((1,), (1,)), ((), ())), preferred_element_type=jnp.float32
        )
        for d in range(some):
            tile = jnp.concatenate([spec[r * S : (r + 1) * S, d * w : (d + 1) * w] for r in range(RL)], axis=1)
            out_ref[d % NZ, q * (some // NZ) + d // NZ] = tile.astype(jnp.bfloat16)
        return carry

    lax.fori_loop(0, cuts, body, 0)


def ref_transform(table, refs):
    return pl.pallas_call(
        ref_kernel,
        in_specs=[away(), whole()],
        out_specs=whole(),
        out_shape=jax.ShapeDtypeStruct((NZ, NY, S, 128), jnp.bfloat16),
        scratch_shapes=[
            pltpu.VMEM((2 * FB, L), jnp.bfloat16),
            pltpu.VMEM((RL * S, L), jnp.bfloat16),
            pltpu.SemaphoreType.DMA((2,)),
        ],
        compiler_params=params(),
        cost_estimate=cost(2 * 2 * FB * L * RL * S, 5_000_000),
    )(table, refs)


def gather_refs(tiles):
    y = lax.axis_index("seg") // NZ
    got = []
    for dy in range(NY):
        slab = lax.dynamic_index_in_dim(tiles, (y + dy) % NY, 1, keepdims=False)
        if dy:
            slab = lax.ppermute(slab, "seg", [(i, (i + dy * NZ) % NSEG) for i in range(NSEG)])
        got.append(slab)
    return lax.all_gather(jnp.stack(got).reshape(NSEG * S, 128), "chan")


def spots(shape, target):
    row = lax.broadcasted_iota(jnp.int32, shape, 0)
    column = lax.broadcasted_iota(jnp.int32, shape, 1)
    return jnp.where(column == target(row), 1.0, 0.0).astype(jnp.bfloat16)


def exact(left, right, dims):
    return lax.dot_general(left, right, (dims, ((), ())), preferred_element_type=jnp.float32).astype(jnp.bfloat16)


def three(a):
    parts = []
    for _ in range(3):
        parts.append(a.astype(jnp.bfloat16))
        a = a - parts[-1].astype(jnp.float32)
    return parts


def invert_kernel(y_ref, ref_ref, out_ref, left, state):
    y = y_ref[0]
    wide = jnp.concatenate([ref_ref[c] for c in range(NCHAN)], axis=1)
    halves = []
    for part in range(2):
        pick = spots(
            (LN * R, NCHAN * 128),
            lambda i: (i // RL) % NCHAN * 128 + i % RL * (2 * LN) + i // R * 2 + part,
        )
        halves.append(exact(pick, wide, ((1,), (1,))))
    real, imag = halves
    put = [spots((NSEG * S, DEPTH), lambda i: (((y - i // (NZ * S) + NY) % NY * NZ + i // S % NZ) * ROWS + part * S + i % S)) for part in range(2)]
    inner = ((1,), (0,))
    upper = exact(real, put[0], inner) + exact(imag, put[1], inner)
    lower = exact(real, put[1], inner) - exact(imag, put[0], inner)
    row = lax.broadcasted_iota(jnp.int32, (R, R), 0)
    column = lax.broadcasted_iota(jnp.int32, (R, R), 1)
    unit = jnp.where(row == column, 1.0, 0.0)
    for k in range(LN):
        rows = slice(k * R, (k + 1) * R)
        both = jnp.concatenate([upper[rows], lower[rows]], axis=0)
        left[k] = both
        own = lax.dot_general(both, upper[rows], (((1,), (1,)), ((), ())), preferred_element_type=jnp.float32)
        state[k] = jnp.concatenate([own[:R], own[R:], unit, jnp.zeros_like(unit)], axis=1)
    row = lax.broadcasted_iota(jnp.int32, (1, R, 1), 1)
    for k in range(R):
        a = state[...]
        pivot = state[:, k : k + 1, :]
        scale = 1.0 / pivot[:, :, k : k + 1]
        turned = jnp.concatenate(
            [-pivot[:, :, R : 2 * R], pivot[:, :, :R], -pivot[:, :, 3 * R :], pivot[:, :, 2 * R : 3 * R]], axis=2
        )
        gain_r = jnp.where(row == k, 0.0, a[:, :, k : k + 1] * scale)
        gain_i = jnp.where(row == k, 0.0, a[:, :, R + k : R + k + 1] * scale)
        state[...] = a - gain_r * pivot - gain_i * turned
    a = state[...]
    row = lax.broadcasted_iota(jnp.int32, (1, R, 4 * R), 1)
    column = lax.broadcasted_iota(jnp.int32, (1, R, 4 * R), 2)
    a = a * (1.0 / jnp.sum(jnp.where(column == row, a, 0.0), axis=2, keepdims=True))
    inv_r, inv_i = a[:, :, 2 * R : 3 * R], a[:, :, 3 * R :]
    for k in range(LN):
        inverse = jnp.concatenate(
            [
                jnp.concatenate([inv_r[k], -inv_i[k]], axis=1),
                jnp.concatenate([inv_i[k], inv_r[k]], axis=1),
            ],
            axis=0,
        )
        terms = jnp.dot(jnp.concatenate(three(inverse), axis=0), left[k], preferred_element_type=jnp.float32)
        terms = terms[: 2 * R] + (terms[2 * R : 4 * R] + terms[4 * R :])
        out_ref[k] = jnp.concatenate(three(terms), axis=0)


def invert(y, refs):
    return pl.pallas_call(
        invert_kernel,
        out_shape=jax.ShapeDtypeStruct((LN, 6 * R, DEPTH), jnp.bfloat16),
        in_specs=[pl.BlockSpec(memory_space=pltpu.SMEM), whole()],
        out_specs=whole(),
        scratch_shapes=[pltpu.VMEM((LN, 2 * R, DEPTH), jnp.bfloat16), pltpu.VMEM((LN, R, 4 * R), jnp.float32)],
        compiler_params=params(),
        cost_estimate=cost(6_000_000_000, 2_000_000),
    )(y, refs)


def apply_kernel(resp_ref, left_ref, out_ref):
    for k in range(LN):
        lines = resp_ref[:, k * ROWS : (k + 1) * ROWS, :].reshape(DEPTH, CL)
        terms = jnp.dot(left_ref[k], lines, preferred_element_type=jnp.float32)
        found = terms[: 2 * R] + (terms[2 * R : 4 * R] + terms[4 * R :])
        out_ref[k, 0] = found[:R]
        out_ref[k, 1] = found[R:]


def apply(lines, left):
    return pl.pallas_call(
        apply_kernel,
        out_shape=jax.ShapeDtypeStruct((LN, 2, R, CL), jnp.float32),
        in_specs=[whole(), whole()],
        out_specs=whole(),
        compiler_params=params(12),
        cost_estimate=cost(2_000_000_000, 4_000_000),
    )(lines, left)


def local(ref_signals, responses):
    table = dft_table()
    tiles = ref_transform(table, ref_signals)
    tiles, responses = lax.optimization_barrier((tiles, responses))
    along_z = [[y * NZ + z for z in range(NZ)] for y in range(NY)]
    tiles = lax.all_to_all(tiles, "seg", 0, 0, axis_index_groups=along_z, tiled=True)
    sent = transform(table, responses)
    sent, tiles = lax.optimization_barrier((sent, tiles))
    lines = lax.all_to_all(sent, "seg", 0, 0, tiled=True)
    y = (lax.axis_index("seg") // NZ).astype(jnp.int32).reshape(1)
    return apply(lines, invert(y, gather_refs(tiles)))


def solution(mesh):
    placed = (P("chan", "seg"), P("chan", "seg"))
    return jax.shard_map(
        local, mesh=mesh, in_specs=placed, out_specs=P("seg", None, None, "chan"), check_vma=False
    )
```
